32 devices in a mesh: tm: 8 (over z, y), zone: 4 (over x, core).
Axes of the slice: x: 2, y: 2, z: 4, core: 2. Of those that a mesh axis runs over, the one named last changes fastest.
Arguments:
- source_field: float32 [64, 8192], P('tm', 'zone'), may hold values from -6 to 6
- remap_weights: bfloat16 [64, 8, 128, 128], P('zone'), may hold values from -0.1875 to 0.1875
- block_columns: int32 [64, 8], P('zone'), may hold values from 0 to 63, all different within a row
- piece_sizes: int32 [4, 8], P('zone'), may hold values from 1 to 1024, 2048 in all within a row
- filter_taps: float32 [1023], replicated, may hold values from -0.1875 to 0.1875
Outputs:
- adjoint_field: float32 [64, 8192], P('tm', 'zone')
The draws below stay inside these ranges and needn't reach their ends.
Inputs may be any that keep to these rules, and one draw needn't show every extreme that they name: `block_columns`: the 8 source blocks of one target block are distinct; every source block feeds some target block. `piece_sizes`: each row sums to 2048; its largest basin has exactly 1024 cells.
All inputs are finite; a program needn't handle non-finite values.
Results may differ from the reference program's by a relative error of at most 0.0038.
Values may be sent and summed in bfloat16 or wider, within the bound.
No kernel may reach another device: no remote copies, remote signals or barrier semaphores. Data moves between devices by JAX's collectives and lax.ppermute only.
A program may use at most 64 MiB of HBM per device.

```python
import math
import jax
import jax.numpy as jnp
import numpy as np
from jax import lax

BS = 128
KB = 8
NB = 64
NC = 8192
NCZ = 2048
SNAPS = 64
TAPS = 1023
MOST = 1024
N_TM = 8
N_ZONE = 4


def block_levels(stream_key, shape, cuts, least, top_value):
    gain = 1.0
    for axis_at, parts in cuts:
        heights = jax.random.uniform(jax.random.fold_in(jax.random.fold_in(stream_key, 6), axis_at), (parts,), jnp.float32, least / len(cuts), top_value / len(cuts))
        gain = gain * jnp.repeat(jnp.exp(heights), shape[axis_at] // parts).reshape((-1,) + (1,) * (len(shape) - 1 - axis_at))
    return gain


def picks_of(own_key, rows, count, top, lift):
    order = jax.random.permutation(jax.random.fold_in(own_key, 1), count)
    pull = order
    for power in range(3):
        pull = pull * pull // count
    pull = pull * lift // count
    tickets = jax.random.randint(jax.random.fold_in(own_key, 2), (rows, count), 0, 4096) + pull
    sure = jax.random.permutation(jax.random.fold_in(own_key, 3), rows)[jnp.arange(count) % rows]
    tickets = jnp.where(jnp.arange(rows)[:, None] == sure[None, :], 1 << 14, tickets)
    merit = tickets * count + jnp.arange(count)
    return lax.top_k(merit.astype(jnp.int32), top)[1].astype(jnp.int32)


def profile(amount, total, limit, lean):
    weights = [(1 << 20) // math.isqrt(grade ** lean) + 1 for grade in range(2, amount + 1)]
    rest, counts = total - limit - (amount - 1), [1] * (amount - 1)
    while rest > 0:
        candidates = [i for i in range(amount - 1) if counts[i] < limit]
        pool, budget = sum([weights[i] for i in candidates]), rest
        for i in candidates:
            extra = min(limit - counts[i], max(1, budget * weights[i] // pool), rest)
            counts[i] = counts[i] + extra
            rest = rest - extra
    return np.array([limit] + counts)


def uneven_parts(stream_key, number_of, total, bound, slope):
    if number_of == 2:
        one = jax.random.randint(stream_key, (), max(1, total - bound), min(bound, total - 1) + 1)
        return jnp.stack([one, total - one])
    tallies = jnp.asarray(profile(number_of, total, bound, slope), jnp.int32)
    twos = (number_of - 1) // 2
    giver, sink = tallies[1:1 + 2 * twos:2], tallies[2:2 + 2 * twos:2]
    margin = jnp.minimum(giver - 1, bound - sink)
    passed = jax.random.randint(jax.random.fold_in(stream_key, 1), (twos,), 0, 1 << 20) % (margin + 1)
    tallies = tallies.at[1:1 + 2 * twos:2].set(giver - passed).at[2:2 + 2 * twos:2].set(sink + passed)
    return tallies[jax.random.permutation(jax.random.fold_in(stream_key, 2), number_of)]


def centred(stream_key, dims, scale, limit, split=(), held_as=jnp.bfloat16):
    entries = scale * jax.random.normal(stream_key, dims, jnp.float32)
    if split:
        entries = entries * block_levels(stream_key, dims, split, -0.22, 0.18)
    return jnp.clip(entries, -limit, limit).astype(held_as)


def setup_inputs(seed: int = 0) -> dict:
    arg_keys = jax.random.split(jax.random.key(seed), 6)
    source_field = centred(arg_keys[0], (SNAPS, NC), 1.0, 6.0, ((0, 8), (1, 4)), jnp.float32)
    remap_weights = centred(arg_keys[1], (NB, KB, BS, BS), (KB * BS) ** -0.5, 0.1875, ((0, 4),))
    block_columns = picks_of(arg_keys[2], NB, NB, KB, 0)
    piece_sizes = jax.vmap(lambda own: uneven_parts(own, N_TM, NCZ, MOST, 2))(jax.random.split(arg_keys[3], N_ZONE)).reshape((N_ZONE, N_TM)).astype(jnp.int32)
    filter_taps = centred(arg_keys[4], (TAPS,), TAPS ** -0.5, 0.1875, (), jnp.float32)
    return dict(source_field=source_field, remap_weights=remap_weights, block_columns=block_columns, piece_sizes=piece_sizes, filter_taps=filter_taps)


def toeplitz_rows(filter_taps, block_rows, span):
    tap_count = filter_taps.shape[0]
    extended = jnp.concatenate([filter_taps, jnp.zeros((span + 1 - tap_count,), filter_taps.dtype)])
    flat = jnp.broadcast_to(extended[None, :], (block_rows, span + 1)).reshape(block_rows * (span + 1))
    return flat[:block_rows * span].reshape(block_rows, span)


def banded(series, filter_taps):
    length, breadth = series.shape
    tap_count = filter_taps.shape[0]
    half_width = (tap_count - 1) // 2
    block_rows = min(512, length)
    toeplitz = toeplitz_rows(filter_taps, block_rows, block_rows + 2 * half_width)
    padded = jnp.pad(series, ((half_width, half_width), (0, 0)))

    def one_block(start):
        window = lax.dynamic_slice_in_dim(padded, start, block_rows + 2 * half_width, 0)
        return jnp.dot(toeplitz, window, precision=lax.Precision.HIGHEST, preferred_element_type=series.dtype)

    starts = (jnp.arange(length // block_rows) * block_rows).astype(jnp.int32)
    return lax.map(one_block, starts).reshape(length, breadth)


def remove_mean(stress, sizes_row):
    cells = stress.shape[1]
    ends = jnp.cumsum(sizes_row)
    begins = ends - sizes_row
    cell_ids = jnp.arange(cells, dtype=jnp.int32)[:, None]
    member = ((cell_ids >= begins[None, :]) & (cell_ids < ends[None, :])).astype(stress.dtype)
    totals = jnp.dot(stress, member, precision=lax.Precision.HIGHEST)
    means = totals / sizes_row.astype(stress.dtype)[None, :]
    return stress - jnp.dot(means, member.T, precision=lax.Precision.HIGHEST)


def reference(source_field, remap_weights, block_columns, piece_sizes, filter_taps):
    xlow = source_field.astype(jnp.bfloat16)
    blocks = xlow.astype(jnp.float32).reshape(SNAPS, NB, BS)

    def forward_row(index):
        picked = blocks[:, block_columns[index]]
        return jnp.einsum("tkb,kab->ta", picked, remap_weights[index].astype(jnp.float32))

    wind = jnp.transpose(lax.map(forward_row, jnp.arange(NB, dtype=jnp.int32)), (1, 0, 2)).reshape(SNAPS, NC)
    stress = wind * jnp.abs(wind)
    pieces = []
    for zone_id in range(N_ZONE):
        part_cells = stress[:, zone_id * NCZ:(zone_id + 1) * NCZ]
        pieces.append(remove_mean(part_cells, piece_sizes[zone_id]))
    anomaly = jnp.concatenate(pieces, axis=1)
    filtered = banded(anomaly, filter_taps)
    flow_low = filtered.astype(jnp.bfloat16).astype(jnp.float32).reshape(SNAPS, NB, BS)

    def backward_row(total, index):
        contrib = jnp.einsum("ta,kab->tkb", flow_low[:, index], remap_weights[index].astype(jnp.float32))
        return total.at[:, block_columns[index]].add(contrib), None

    start_total = jnp.zeros((SNAPS, NB, BS), jnp.float32)
    total, unused = lax.scan(backward_row, start_total, jnp.arange(NB, dtype=jnp.int32))
    return total.reshape(SNAPS, NC)
```

```python
import functools
import jax
import jax.numpy as jnp
from jax import lax
from jax.experimental import pallas as pl
from jax.experimental.pallas import tpu as pltpu
from jax.sharding import PartitionSpec as P

VMEM = pl.BlockSpec(memory_space=pltpu.VMEM)
SMEM = pl.BlockSpec(memory_space=pltpu.SMEM)
HBM = pl.BlockSpec(memory_space=pltpu.HBM)
NT = (((1,), (1,)), ((), ()))
LIMIT = 16 * 2**20
DIRECT = 8
NEAR = 4


def three_parts(value):
    high = value.astype(jnp.bfloat16)
    rest = value - high.astype(jnp.float32)
    middle = rest.astype(jnp.bfloat16)
    low = (rest - middle.astype(jnp.float32)).astype(jnp.bfloat16)
    return high, middle, low


def ahead(snapshots, half_width, width):
    return -(-max(0, snapshots + width - half_width) // 128) * 128


def prepare_kernel(where_ref, sizes_hbm, taps_hbm, weights_ref, *refs):
    held_ref, rows_ref, member_ref, count_ref, line_ref, sizes_ref, taps_ref, sems = refs
    taps_total = taps_hbm.shape[1]
    parts = sems.shape[0] - 2
    taps_copy = pltpu.make_async_copy(taps_hbm, taps_ref, sems.at[parts])
    sizes_copy = pltpu.make_async_copy(sizes_hbm, sizes_ref, sems.at[parts + 1])
    taps_copy.start()
    sizes_copy.start()
    each = weights_ref.shape[0] // parts
    copies = [
        pltpu.make_async_copy(
            weights_ref.at[pl.ds(n * each, each)], held_ref.at[pl.ds(n * each, each)], sems.at[n]
        )
        for n in range(parts)
    ]
    for copy in copies:
        copy.start()

    rows, width = line_ref.shape
    half_width = (taps_total - 1) // 2
    steps = rows_ref.shape[0] // rows
    before = ahead(steps * rows_ref.shape[1], half_width, rows_ref.shape[1])
    line_ref[...] = jnp.zeros_like(line_ref)
    taps_copy.wait()
    line_ref[:, before : before + taps_total] = jnp.broadcast_to(
        taps_ref[...], (rows, taps_total)
    )
    line = line_ref[...]
    row_ids = lax.broadcasted_iota(jnp.int32, (rows, 1), 0)
    slanted = line
    for r in range(1, rows):
        slanted = jnp.where(row_ids == r, pltpu.roll(line, r, 1), slanted)
    line_ref[...] = slanted
    near = rows_ref.shape[1] // rows
    lanes = lax.broadcasted_iota(jnp.int32, (rows, near * rows), 1)
    at = where_ref[1]
    for step in range(steps):
        target = at ^ (near * step) if steps <= DIRECT else near * step + (at & (near - 1))
        found = jnp.zeros((rows, near * rows), jnp.float32)
        for n in range(near):
            base = ((at ^ n) - target) * rows + half_width - n * rows + before
            first = pl.multiple_of((base >> 7) << 7, 128)
            window = line_ref[:, pl.ds(first, 256)]
            turned = pltpu.roll(window, (256 - (base & 127)) & 255, 1)
            found = jnp.where(lanes >= n * rows, turned[:, : near * rows], found)
        rows_ref[step * rows : (step + 1) * rows, :] = found

    sizes_copy.wait()
    basins, cells = member_ref.shape
    cell_ids = lax.broadcasted_iota(jnp.int32, (1, cells), 1)
    basin_ids = jnp.zeros((1, cells), jnp.int32)
    basin_lanes = lax.broadcasted_iota(jnp.int32, (1, basins), 1)
    counts = jnp.zeros((1, basins), jnp.int32)
    end = 0
    for g in range(basins):
        counts = jnp.where(basin_lanes == g, sizes_ref[0, g], counts)
        if g:
            basin_ids += (cell_ids >= end).astype(jnp.int32)
        end = end + sizes_ref[0, g]
    member = lax.broadcasted_iota(jnp.int32, (basins, cells), 0) == basin_ids
    member_ref[...] = member.astype(jnp.float32).astype(jnp.bfloat16)
    count_ref[...] = counts.astype(jnp.float32)
    for copy in copies:
        copy.wait()


def prepare(where, sizes, filter_taps, weights, steps, near, rows):
    taps_total = filter_taps.shape[0]
    half_width = (taps_total - 1) // 2
    snapshots = near * steps * rows
    width = ahead(snapshots, half_width, near * rows) + max(taps_total + rows, half_width + snapshots) + 256
    width = -(-width // 128) * 128
    basins = sizes.shape[1]
    cells = weights.shape[0] * weights.shape[2]
    return pl.pallas_call(
        prepare_kernel,
        out_shape=[
            jax.ShapeDtypeStruct(weights.shape, weights.dtype),
            jax.ShapeDtypeStruct((steps * rows, near * rows), jnp.float32),
            jax.ShapeDtypeStruct((basins, cells), jnp.bfloat16),
            jax.ShapeDtypeStruct((1, basins), jnp.float32),
        ],
        in_specs=[SMEM, HBM, HBM, HBM],
        out_specs=[VMEM] * 4,
        scratch_shapes=[
            pltpu.VMEM((rows, width), jnp.float32),
            pltpu.SMEM(sizes.shape, sizes.dtype),
            pltpu.VMEM((1, taps_total), jnp.float32),
            pltpu.SemaphoreType.DMA((6,)),
        ],
        compiler_params=pltpu.CompilerParams(vmem_limit_bytes=46 * 2**20),
        cost_estimate=pl.CostEstimate(flops=0, bytes_accessed=8 * 2**20, transcendentals=0),
        name="prepare",
    )(where, sizes, filter_taps.reshape(1, -1), weights)


def remap_kernel(zones, where_ref, columns_ref, member_ref, count_ref, *refs):
    x_refs, (weights_ref, *refs) = refs[:zones], refs[zones:]
    c_refs, (blocks_ref, total_ref) = refs[:zones], refs[zones:]
    zone_blocks, slots, size, _ = weights_ref.shape
    rows = x_refs[0].shape[0]
    me = where_ref[0]
    for step in range(zones):
        first = (me ^ step) * zone_blocks
        for b in range(zone_blocks):
            blocks_ref[first + b] = x_refs[step][:, b * size : (b + 1) * size].astype(jnp.float32)
    total_ref[...] = jnp.zeros_like(total_ref)

    pieces = []
    for i in range(zone_blocks):
        picked = jnp.concatenate([blocks_ref[columns_ref[k, i]] for k in range(slots)], axis=1)
        wide = jnp.concatenate([weights_ref[i, k] for k in range(slots)], axis=1)
        wind = lax.dot_general(
            picked.astype(jnp.bfloat16), wide, NT, preferred_element_type=jnp.float32
        )
        pieces.append(wind * jnp.abs(wind))
    stress = jnp.concatenate(pieces, axis=1)

    member = member_ref[...]
    parts = lax.dot_general(
        jnp.concatenate(three_parts(stress), axis=0), member, NT, preferred_element_type=jnp.float32
    )
    totals = parts[:rows] + parts[rows : 2 * rows] + parts[2 * rows :]
    means = totals / count_ref[...]
    spread = jnp.dot(
        jnp.concatenate(three_parts(means), axis=0), member, preferred_element_type=jnp.float32
    )
    anomaly = stress - (spread[:rows] + spread[rows : 2 * rows] + spread[2 * rows :])

    high = anomaly.astype(jnp.bfloat16)
    low = (anomaly - high.astype(jnp.float32)).astype(jnp.bfloat16)
    both = jnp.concatenate([high, low], axis=0)
    for i in range(zone_blocks):
        wide = jnp.concatenate([weights_ref[i, k] for k in range(slots)], axis=1)
        back = jnp.dot(
            both[:, i * size : (i + 1) * size], wide, preferred_element_type=jnp.float32
        )
        back = back[:rows] + back[rows:]
        for k in range(slots):
            column = columns_ref[k, i]
            total_ref[column] += back[:, k * size : (k + 1) * size]
    for step in range(zones):
        first = (me ^ step) * zone_blocks
        for b in range(zone_blocks):
            c_refs[step][:, b * size : (b + 1) * size] = total_ref[first + b].astype(
                c_refs[step].dtype
            )


def remap(where, columns, member, counts, xs, weights):
    zones = len(xs)
    rows, cells = xs[0].shape
    all_blocks = zones * weights.shape[0]
    size = weights.shape[2]
    outs = [
        jax.ShapeDtypeStruct((rows, cells), jnp.bfloat16 if step else jnp.float32)
        for step in range(zones)
    ]
    return pl.pallas_call(
        functools.partial(remap_kernel, zones),
        out_shape=outs,
        in_specs=[SMEM, SMEM] + [VMEM] * (3 + zones),
        out_specs=[VMEM] * zones,
        scratch_shapes=[
            pltpu.VMEM((all_blocks, rows, size), jnp.float32),
            pltpu.VMEM((all_blocks, rows, size), jnp.float32),
        ],
        compiler_params=pltpu.CompilerParams(vmem_limit_bytes=LIMIT),
        cost_estimate=pl.CostEstimate(flops=10**8, bytes_accessed=8 * 2**20, transcendentals=0),
        name="remap",
    )(where, columns, member, counts, *xs, weights)


def gather_kernel(*refs):
    *parts, total_ref, low_ref = refs
    total = sum(r[...].astype(jnp.float32) for r in parts)
    total_ref[...] = total
    low_ref[...] = total.astype(low_ref.dtype)


def add_zones(parts):
    return pl.pallas_call(
        gather_kernel,
        out_shape=[jax.ShapeDtypeStruct(parts[0].shape, d) for d in (jnp.float32, jnp.bfloat16)],
        in_specs=[VMEM] * len(parts),
        out_specs=[VMEM] * 2,
        compiler_params=pltpu.CompilerParams(vmem_limit_bytes=LIMIT),
        name="add_zones",
    )(*parts)


def filter_kernel(near, taps_ref, *refs):
    values, outs = refs[:near], refs[near:]
    rows = values[0].shape[0]
    together = jnp.concatenate([r[...].astype(jnp.float32) for r in values], axis=0)
    result = jnp.dot(
        taps_ref[...], together, precision=lax.Precision.HIGHEST, preferred_element_type=jnp.float32
    )
    if len(outs) == 1:
        outs[0][...] = result.astype(outs[0].dtype)
        return
    for step, out in enumerate(outs):
        out[...] = result[step * rows : (step + 1) * rows].astype(out.dtype)


def time_filter(taps, values):
    rows, cells = values[0].shape
    steps = taps.shape[0] // rows
    if steps <= DIRECT:
        outs = [
            jax.ShapeDtypeStruct((rows, cells), jnp.bfloat16 if step else jnp.float32)
            for step in range(steps)
        ]
    else:
        outs = [jax.ShapeDtypeStruct((steps * rows, cells), jnp.bfloat16)]
    return pl.pallas_call(
        functools.partial(filter_kernel, len(values)),
        out_shape=outs,
        in_specs=[VMEM] * (1 + len(values)),
        out_specs=[VMEM] * len(outs),
        compiler_params=pltpu.CompilerParams(vmem_limit_bytes=LIMIT),
        name="time_filter",
    )(taps, *values)


def sum_kernel(*refs):
    refs[-1][...] = sum(r[...].astype(jnp.float32) for r in refs[:-1])


def add_up(parts):
    return pl.pallas_call(
        sum_kernel,
        out_shape=jax.ShapeDtypeStruct(parts[0].shape, jnp.float32),
        in_specs=[VMEM] * len(parts),
        out_specs=VMEM,
        compiler_params=pltpu.CompilerParams(vmem_limit_bytes=LIMIT),
        name="add_up",
    )(*parts)


def swap(value, axis, by):
    return lax.ppermute(value, axis, [(i, i ^ by) for i in range(lax.axis_size(axis))])


def shards(source_field, remap_weights, block_columns, piece_sizes, filter_taps):
    rows, cells = source_field.shape
    zones, owners = lax.axis_size("zone"), lax.axis_size("tm")
    near = min(NEAR, owners)
    steps = owners // near
    where = jnp.stack([lax.axis_index("zone"), lax.axis_index("tm")])
    xlow = source_field.astype(jnp.bfloat16)
    xs = [xlow] + [swap(xlow, "zone", step) for step in range(1, zones)]
    held, taps, member, counts = prepare(
        where, piece_sizes, filter_taps, remap_weights, steps, near, rows
    )
    sent = remap(where, block_columns.T, member, counts, xs, held)

    summed, low = add_zones(
        [sent[0]] + [swap(sent[step], "zone", step) for step in range(1, zones)]
    )
    parts = time_filter(taps, [summed] + [swap(low, "tm", n) for n in range(1, near)])
    if steps <= DIRECT:
        last = [parts[0]] + [swap(parts[step], "tm", near * step) for step in range(1, steps)]
        return add_up(last)
    groups = [list(range(side, owners, near)) for side in range(near)]
    parts = lax.all_to_all(
        parts[0].reshape(steps, rows, cells), "tm", 0, 0, axis_index_groups=groups
    )
    return parts.astype(jnp.float32).sum(axis=0)


def solution(mesh):
    return jax.shard_map(
        shards,
        mesh=mesh,
        in_specs=(
            P("tm", "zone"),
            P("zone", None, None, None),
            P("zone", None),
            P("zone", None),
            P(),
        ),
        out_specs=P("tm", "zone"),
        check_vma=False,
    )
```

```python
import functools
import jax
import jax.numpy as jnp
from jax import lax
from jax.experimental import pallas as pl
from jax.experimental.pallas import tpu as pltpu
from jax.sharding import PartitionSpec as P

VMEM = pl.BlockSpec(memory_space=pltpu.VMEM)
HBM = pl.BlockSpec(memory_space=pltpu.HBM)
NT = (((1,), (1,)), ((), ()))
LIMIT = 16 * 2**20
DIRECT = 8
NEAR = 4


def three_parts(value):
    high = value.astype(jnp.bfloat16)
    rest = value - high.astype(jnp.float32)
    middle = rest.astype(jnp.bfloat16)
    low = (rest - middle.astype(jnp.float32)).astype(jnp.bfloat16)
    return high, middle, low


def ahead(snapshots, half_width, width):
    return -(-max(0, snapshots + width - half_width) // 128) * 128


def hold_kernel(weights_ref, held_ref, turned_ref, sems):
    zone_blocks, slots, _, _ = weights_ref.shape
    parts = sems.shape[0]
    each = zone_blocks // parts
    copies = [
        pltpu.make_async_copy(
            weights_ref.at[pl.ds(n * each, each)], held_ref.at[pl.ds(n * each, each)], sems.at[n]
        )
        for n in range(parts)
    ]
    for copy in copies:
        copy.start()
    for n, copy in enumerate(copies):
        copy.wait()
        for i in range(n * each, min((n + 1) * each, turned_ref.shape[0])):
            for k in range(slots):
                turned_ref[i, k] = held_ref[i, k].T


def hold(weights):
    zone_blocks = weights.shape[0]
    turned = zone_blocks - zone_blocks // 4
    return pl.pallas_call(
        hold_kernel,
        out_shape=[
            jax.ShapeDtypeStruct((count, *weights.shape[1:]), weights.dtype)
            for count in (zone_blocks, turned)
        ],
        in_specs=[HBM],
        out_specs=[VMEM] * 2,
        scratch_shapes=[pltpu.SemaphoreType.DMA((min(4, weights.shape[0]),))],
        compiler_params=pltpu.CompilerParams(vmem_limit_bytes=43 * 2**20),
        cost_estimate=pl.CostEstimate(flops=0, bytes_accessed=8 * 2**20, transcendentals=0),
        name="hold",
    )(weights)


def prepare_kernel(where_ref, taps_ref, rows_ref, line_ref):
    taps_total = taps_ref.shape[1]
    rows, width = line_ref.shape
    half_width = (taps_total - 1) // 2
    steps = rows_ref.shape[0] // rows
    before = ahead(steps * rows_ref.shape[1], half_width, rows_ref.shape[1])
    line_ref[...] = jnp.zeros_like(line_ref)
    line_ref[:, before : before + taps_total] = jnp.broadcast_to(
        taps_ref[...], (rows, taps_total)
    )
    line = line_ref[...]
    row_ids = lax.broadcasted_iota(jnp.int32, (rows, 1), 0)
    slanted = line
    for r in range(1, rows):
        slanted = jnp.where(row_ids == r, pltpu.roll(line, r, 1), slanted)
    line_ref[...] = slanted
    near = rows_ref.shape[1] // rows
    lanes = lax.broadcasted_iota(jnp.int32, (rows, near * rows), 1)
    at = where_ref[0, 1]
    for step in range(steps):
        target = at ^ (near * step) if steps <= DIRECT else near * step + (at & (near - 1))
        found = jnp.zeros((rows, near * rows), jnp.float32)
        for n in range(near):
            base = ((at ^ n) - target) * rows + half_width - n * rows + before
            first = pl.multiple_of((base >> 7) << 7, 128)
            window = line_ref[:, pl.ds(first, 256)]
            turned = pltpu.roll(window, (256 - (base & 127)) & 255, 1)
            found = jnp.where(lanes >= n * rows, turned[:, : near * rows], found)
        rows_ref[step * rows : (step + 1) * rows, :] = found


def prepare(where, filter_taps, steps, near, rows):
    taps_total = filter_taps.shape[0]
    half_width = (taps_total - 1) // 2
    snapshots = near * steps * rows
    width = ahead(snapshots, half_width, near * rows) + max(taps_total + rows, half_width + snapshots) + 256
    width = -(-width // 128) * 128
    return pl.pallas_call(
        prepare_kernel,
        out_shape=jax.ShapeDtypeStruct((steps * rows, near * rows), jnp.float32),
        in_specs=[VMEM] * 2,
        out_specs=VMEM,
        scratch_shapes=[pltpu.VMEM((rows, width), jnp.float32)],
        compiler_params=pltpu.CompilerParams(vmem_limit_bytes=LIMIT),
        cost_estimate=pl.CostEstimate(flops=0, bytes_accessed=4 * 2**20, transcendentals=0),
        name="prepare",
    )(where, filter_taps.reshape(1, -1))


def remap_kernel(zones, where_ref, columns_ref, sizes_ref, *refs):
    x_refs, (weights_ref, turned_ref, *refs) = refs[:zones], refs[zones:]
    c_refs, (blocks_ref, total_ref) = refs[:zones], refs[zones:]
    zone_blocks, slots, size, _ = weights_ref.shape
    rows = x_refs[0].shape[0]
    me = where_ref[0, 0]
    for step in range(zones):
        first = (me ^ (zones - step if step else 0)) * zone_blocks
        for b in range(zone_blocks):
            blocks_ref[first + b] = x_refs[step][:, b * size : (b + 1) * size].astype(jnp.float32)
    total_ref[...] = jnp.zeros_like(total_ref)

    pieces = []
    for i in range(zone_blocks):
        picked = jnp.concatenate([blocks_ref[columns_ref[k, i]] for k in range(slots)], axis=1)
        picked = picked.astype(jnp.bfloat16)
        if i < turned_ref.shape[0]:
            block = turned_ref[i].reshape(slots * size, size)
            wind = jnp.dot(picked, block, preferred_element_type=jnp.float32)
        else:
            wide = jnp.concatenate([weights_ref[i, k] for k in range(slots)], axis=1)
            wind = lax.dot_general(picked, wide, NT, preferred_element_type=jnp.float32)
        pieces.append(wind * jnp.abs(wind))
    stress = jnp.concatenate(pieces, axis=1)

    basins, cells = sizes_ref.shape[1], x_refs[0].shape[1]
    cell_ids = lax.broadcasted_iota(jnp.int32, (1, cells), 1)
    basin_ids = jnp.zeros((1, cells), jnp.int32)
    basin_lanes = lax.broadcasted_iota(jnp.int32, (1, basins), 1)
    counts = jnp.zeros((1, basins), jnp.int32)
    end = 0
    for g in range(basins):
        counts = jnp.where(basin_lanes == g, sizes_ref[0, g], counts)
        if g:
            basin_ids += (cell_ids >= end).astype(jnp.int32)
        end = end + sizes_ref[0, g]
    member = lax.broadcasted_iota(jnp.int32, (basins, cells), 0) == basin_ids
    member = member.astype(jnp.float32).astype(jnp.bfloat16)
    parts = lax.dot_general(
        jnp.concatenate(three_parts(stress), axis=0), member, NT, preferred_element_type=jnp.float32
    )
    totals = parts[:rows] + parts[rows : 2 * rows] + parts[2 * rows :]
    means = totals / counts.astype(jnp.float32)
    spread = jnp.dot(
        jnp.concatenate(three_parts(means), axis=0), member, preferred_element_type=jnp.float32
    )
    anomaly = stress - (spread[:rows] + spread[rows : 2 * rows] + spread[2 * rows :])

    high = anomaly.astype(jnp.bfloat16)
    low = (anomaly - high.astype(jnp.float32)).astype(jnp.bfloat16)
    both = jnp.concatenate([high, low], axis=0)
    for i in range(zone_blocks):
        wide = jnp.concatenate([weights_ref[i, k] for k in range(slots)], axis=1)
        back = jnp.dot(
            both[:, i * size : (i + 1) * size], wide, preferred_element_type=jnp.float32
        )
        back = back[:rows] + back[rows:]
        targets = [columns_ref[k, i] for k in range(slots)]
        before = [total_ref[column] for column in targets]
        for k in range(slots):
            total_ref[targets[k]] = before[k] + back[:, k * size : (k + 1) * size]
    for step in range(zones):
        first = (me ^ step) * zone_blocks
        for b in range(zone_blocks):
            c_refs[step][:, b * size : (b + 1) * size] = total_ref[first + b].astype(
                c_refs[step].dtype
            )


def remap(where, columns, sizes, xs, weights, turned):
    zones = len(xs)
    rows, cells = xs[0].shape
    all_blocks = zones * weights.shape[0]
    size = weights.shape[2]
    outs = [
        jax.ShapeDtypeStruct((rows, cells), jnp.bfloat16 if step else jnp.float32)
        for step in range(zones)
    ]
    return pl.pallas_call(
        functools.partial(remap_kernel, zones),
        out_shape=outs,
        in_specs=[VMEM] * (5 + zones),
        out_specs=[VMEM] * zones,
        scratch_shapes=[
            pltpu.VMEM((all_blocks, rows, size), jnp.float32),
            pltpu.VMEM((all_blocks, rows, size), jnp.float32),
        ],
        compiler_params=pltpu.CompilerParams(vmem_limit_bytes=LIMIT),
        cost_estimate=pl.CostEstimate(flops=10**8, bytes_accessed=8 * 2**20, transcendentals=0),
        name="remap",
    )(where, columns, sizes, *xs, weights, turned)


def gather_kernel(taps_ref, *refs):
    *parts, total_ref, low_ref = refs
    del taps_ref
    total = sum(r[...].astype(jnp.float32) for r in parts)
    total_ref[...] = total
    low_ref[...] = total.astype(low_ref.dtype)


def add_zones(taps, parts):
    return pl.pallas_call(
        gather_kernel,
        out_shape=[jax.ShapeDtypeStruct(parts[0].shape, d) for d in (jnp.float32, jnp.bfloat16)],
        in_specs=[VMEM] * (1 + len(parts)),
        out_specs=[VMEM] * 2,
        compiler_params=pltpu.CompilerParams(vmem_limit_bytes=LIMIT),
        name="add_zones",
    )(taps, *parts)


def filter_kernel(near, taps_ref, *refs):
    values, outs = refs[:near], refs[near:]
    rows = values[0].shape[0]
    values = [values[0], *values[:0:-1]]
    together = jnp.concatenate([r[...].astype(jnp.float32) for r in values], axis=0)
    result = jnp.dot(
        taps_ref[...], together, precision=lax.Precision.HIGHEST, preferred_element_type=jnp.float32
    )
    if len(outs) == 1:
        outs[0][...] = result.astype(outs[0].dtype)
        return
    for step, out in enumerate(outs):
        out[...] = result[step * rows : (step + 1) * rows].astype(out.dtype)


def time_filter(taps, values):
    rows, cells = values[0].shape
    steps = taps.shape[0] // rows
    if steps <= DIRECT:
        outs = [
            jax.ShapeDtypeStruct((rows, cells), jnp.bfloat16 if step else jnp.float32)
            for step in range(steps)
        ]
    else:
        outs = [jax.ShapeDtypeStruct((steps * rows, cells), jnp.bfloat16)]
    return pl.pallas_call(
        functools.partial(filter_kernel, len(values)),
        out_shape=outs,
        in_specs=[VMEM] * (1 + len(values)),
        out_specs=[VMEM] * len(outs),
        compiler_params=pltpu.CompilerParams(vmem_limit_bytes=LIMIT),
        name="time_filter",
    )(taps, *values)


def sum_kernel(*refs):
    refs[-1][...] = sum(r[...].astype(jnp.float32) for r in refs[:-1])


def add_up(parts):
    return pl.pallas_call(
        sum_kernel,
        out_shape=jax.ShapeDtypeStruct(parts[0].shape, jnp.float32),
        in_specs=[VMEM] * len(parts),
        out_specs=VMEM,
        compiler_params=pltpu.CompilerParams(vmem_limit_bytes=LIMIT),
        name="add_up",
    )(*parts)


def swap(value, axis, by):
    return lax.ppermute(value, axis, [(i, i ^ by) for i in range(lax.axis_size(axis))])


def shards(source_field, remap_weights, block_columns, piece_sizes, filter_taps):
    rows, cells = source_field.shape
    zones, owners = lax.axis_size("zone"), lax.axis_size("tm")
    near = min(NEAR, owners)
    steps = owners // near
    where = jnp.stack([lax.axis_index("zone"), lax.axis_index("tm")]).reshape(1, 2)
    xlow = source_field.astype(jnp.bfloat16)
    xs = [xlow] + [swap(xlow, "zone", step) for step in range(zones - 1, 0, -1)]
    held, turned = hold(remap_weights)
    sent = remap(where, block_columns.T, piece_sizes, xs, held, turned)
    taps = prepare(where, filter_taps, steps, near, rows)
    summed, low = add_zones(
        taps, [sent[0]] + [swap(sent[step], "zone", step) for step in range(zones - 1, 0, -1)]
    )
    others = [swap(low, "tm", n) for n in range(near - 1, 0, -1)]
    parts = time_filter(taps, [summed] + others)
    if steps <= DIRECT:
        last = [parts[0]] + [swap(parts[step], "tm", near * step) for step in range(1, steps)]
        return add_up(last)
    groups = [list(range(side, owners, near)) for side in range(near)]
    parts = lax.all_to_all(
        parts[0].reshape(steps, rows, cells), "tm", 0, 0, axis_index_groups=groups
    )
    return parts.astype(jnp.float32).sum(axis=0)


def solution(mesh):
    return jax.shard_map(
        shards,
        mesh=mesh,
        in_specs=(
            P("tm", "zone"),
            P("zone", None, None, None),
            P("zone", None),
            P("zone", None),
            P(),
        ),
        out_specs=P("tm", "zone"),
        check_vma=False,
    )
```

```python
import functools
import jax
import jax.numpy as jnp
from jax import lax
from jax.experimental import pallas as pl
from jax.experimental.pallas import tpu as pltpu
from jax.sharding import PartitionSpec as P

VMEM = pl.BlockSpec(memory_space=pltpu.VMEM)
HBM = pl.BlockSpec(memory_space=pltpu.HBM)
NT = (((1,), (1,)), ((), ()))
LIMIT = 16 * 2**20
DIRECT = 8
NEAR = 4


def three_parts(value):
    high = value.astype(jnp.bfloat16)
    rest = value - high.astype(jnp.float32)
    middle = rest.astype(jnp.bfloat16)
    low = (rest - middle.astype(jnp.float32)).astype(jnp.bfloat16)
    return high, middle, low


def ahead(snapshots, half_width, width):
    return -(-max(0, snapshots + width - half_width) // 128) * 128


def hold_kernel(weights_ref, held_ref, turned_ref, sems):
    zone_blocks, slots, _, _ = weights_ref.shape
    parts = sems.shape[0]
    each = zone_blocks // parts
    copies = [
        pltpu.make_async_copy(
            weights_ref.at[pl.ds(n * each, each)], held_ref.at[pl.ds(n * each, each)], sems.at[n]
        )
        for n in range(parts)
    ]
    for copy in copies:
        copy.start()
    for n, copy in enumerate(copies):
        copy.wait()
        for i in range(n * each, min((n + 1) * each, turned_ref.shape[0])):
            for k in range(slots):
                turned_ref[i, k] = held_ref[i, k].T


def hold(weights):
    zone_blocks = weights.shape[0]
    turned = zone_blocks - zone_blocks // 4
    return pl.pallas_call(
        hold_kernel,
        out_shape=[
            jax.ShapeDtypeStruct((count, *weights.shape[1:]), weights.dtype)
            for count in (zone_blocks, turned)
        ],
        in_specs=[HBM],
        out_specs=[VMEM] * 2,
        scratch_shapes=[pltpu.SemaphoreType.DMA((min(4, weights.shape[0]),))],
        compiler_params=pltpu.CompilerParams(vmem_limit_bytes=43 * 2**20),
        cost_estimate=pl.CostEstimate(flops=0, bytes_accessed=8 * 2**20, transcendentals=0),
        name="hold",
    )(weights)


def prepare_kernel(where_ref, taps_ref, rows_ref, line_ref):
    taps_total = taps_ref.shape[1]
    rows, width = line_ref.shape
    half_width = (taps_total - 1) // 2
    steps = rows_ref.shape[0] // rows
    before = ahead(steps * rows_ref.shape[1], half_width, rows_ref.shape[1])
    line_ref[...] = jnp.zeros_like(line_ref)
    line_ref[:, before : before + taps_total] = jnp.broadcast_to(
        taps_ref[...], (rows, taps_total)
    )
    line = line_ref[...]
    row_ids = lax.broadcasted_iota(jnp.int32, (rows, 1), 0)
    slanted = line
    for r in range(1, rows):
        slanted = jnp.where(row_ids == r, pltpu.roll(line, r, 1), slanted)
    line_ref[...] = slanted
    near = rows_ref.shape[1] // rows
    lanes = lax.broadcasted_iota(jnp.int32, (rows, near * rows), 1)
    at = where_ref[0, 1]
    for step in range(steps):
        target = at ^ (near * step) if steps <= DIRECT else near * step + (at & (near - 1))
        found = jnp.zeros((rows, near * rows), jnp.float32)
        for n in range(near):
            base = ((at ^ n) - target) * rows + half_width - n * rows + before
            first = pl.multiple_of((base >> 7) << 7, 128)
            window = line_ref[:, pl.ds(first, 256)]
            turned = pltpu.roll(window, (256 - (base & 127)) & 255, 1)
            found = jnp.where(lanes >= n * rows, turned[:, : near * rows], found)
        rows_ref[step * rows : (step + 1) * rows, :] = found


def prepare(where, filter_taps, steps, near, rows):
    taps_total = filter_taps.shape[0]
    half_width = (taps_total - 1) // 2
    snapshots = near * steps * rows
    width = ahead(snapshots, half_width, near * rows) + max(taps_total + rows, half_width + snapshots) + 256
    width = -(-width // 128) * 128
    return pl.pallas_call(
        prepare_kernel,
        out_shape=jax.ShapeDtypeStruct((steps * rows, near * rows), jnp.float32),
        in_specs=[VMEM] * 2,
        out_specs=VMEM,
        scratch_shapes=[pltpu.VMEM((rows, width), jnp.float32)],
        compiler_params=pltpu.CompilerParams(vmem_limit_bytes=LIMIT),
        cost_estimate=pl.CostEstimate(flops=0, bytes_accessed=4 * 2**20, transcendentals=0),
        name="prepare",
    )(where, filter_taps.reshape(1, -1))


def remap_kernel(zones, where_ref, columns_ref, sizes_ref, *refs):
    x_refs, (weights_ref, turned_ref, *refs) = refs[:zones], refs[zones:]
    c_refs, (blocks_ref, total_ref) = refs[:zones], refs[zones:]
    zone_blocks, slots, size, _ = weights_ref.shape
    rows = x_refs[0].shape[0]
    me = where_ref[0, 0]
    for step in range(zones):
        first = (me ^ (zones - step if step else 0)) * zone_blocks
        for b in range(zone_blocks):
            blocks_ref[first + b] = x_refs[step][:, b * size : (b + 1) * size].astype(jnp.float32)
    total_ref[...] = jnp.zeros_like(total_ref)

    pieces = []
    for i in range(zone_blocks):
        picked = jnp.concatenate([blocks_ref[columns_ref[k, i]] for k in range(slots)], axis=1)
        picked = picked.astype(jnp.bfloat16)
        if i < turned_ref.shape[0]:
            block = turned_ref[i].reshape(slots * size, size)
            wind = jnp.dot(picked, block, preferred_element_type=jnp.float32)
        else:
            wide = jnp.concatenate([weights_ref[i, k] for k in range(slots)], axis=1)
            wind = lax.dot_general(picked, wide, NT, preferred_element_type=jnp.float32)
        pieces.append(wind * jnp.abs(wind))
    stress = jnp.concatenate(pieces, axis=1)

    basins, cells = sizes_ref.shape[1], x_refs[0].shape[1]
    cell_ids = lax.broadcasted_iota(jnp.int32, (1, cells), 1)
    basin_ids = jnp.zeros((1, cells), jnp.int32)
    basin_lanes = lax.broadcasted_iota(jnp.int32, (1, basins), 1)
    counts = jnp.zeros((1, basins), jnp.int32)
    end = 0
    for g in range(basins):
        counts = jnp.where(basin_lanes == g, sizes_ref[0, g], counts)
        if g:
            basin_ids += (cell_ids >= end).astype(jnp.int32)
        end = end + sizes_ref[0, g]
    member = lax.broadcasted_iota(jnp.int32, (basins, cells), 0) == basin_ids
    member = member.astype(jnp.float32).astype(jnp.bfloat16)
    parts = lax.dot_general(
        jnp.concatenate(three_parts(stress), axis=0), member, NT, preferred_element_type=jnp.float32
    )
    totals = parts[:rows] + parts[rows : 2 * rows] + parts[2 * rows :]
    means = totals / counts.astype(jnp.float32)
    spread = jnp.dot(
        jnp.concatenate(three_parts(means), axis=0), member, preferred_element_type=jnp.float32
    )
    anomaly = stress - (spread[:rows] + spread[rows : 2 * rows] + spread[2 * rows :])

    high = anomaly.astype(jnp.bfloat16)
    low = (anomaly - high.astype(jnp.float32)).astype(jnp.bfloat16)
    both = jnp.concatenate([high, low], axis=0)
    for i in range(zone_blocks):
        wide = jnp.concatenate([weights_ref[i, k] for k in range(slots)], axis=1)
        back = jnp.dot(
            both[:, i * size : (i + 1) * size], wide, preferred_element_type=jnp.float32
        )
        back = back[:rows] + back[rows:]
        targets = [columns_ref[k, i] for k in range(slots)]
        before = [total_ref[column] for column in targets]
        for k in range(slots):
            total_ref[targets[k]] = before[k] + back[:, k * size : (k + 1) * size]
    for step in range(zones):
        first = (me ^ step) * zone_blocks
        for b in range(zone_blocks):
            c_refs[step][:, b * size : (b + 1) * size] = total_ref[first + b].astype(
                c_refs[step].dtype
            )


def remap(where, columns, sizes, xs, weights, turned):
    zones = len(xs)
    rows, cells = xs[0].shape
    all_blocks = zones * weights.shape[0]
    size = weights.shape[2]
    outs = [
        jax.ShapeDtypeStruct((rows, cells), jnp.bfloat16 if step else jnp.float32)
        for step in range(zones)
    ]
    return pl.pallas_call(
        functools.partial(remap_kernel, zones),
        out_shape=outs,
        in_specs=[VMEM] * (5 + zones),
        out_specs=[VMEM] * zones,
        scratch_shapes=[
            pltpu.VMEM((all_blocks, rows, size), jnp.float32),
            pltpu.VMEM((all_blocks, rows, size), jnp.float32),
        ],
        compiler_params=pltpu.CompilerParams(vmem_limit_bytes=LIMIT),
        cost_estimate=pl.CostEstimate(flops=10**8, bytes_accessed=8 * 2**20, transcendentals=0),
        name="remap",
    )(where, columns, sizes, *xs, weights, turned)


def gather_kernel(taps_ref, *refs):
    *parts, low_ref = refs
    del taps_ref
    low_ref[...] = sum(r[...].astype(jnp.float32) for r in parts).astype(low_ref.dtype)


def add_zones(taps, parts):
    return pl.pallas_call(
        gather_kernel,
        out_shape=jax.ShapeDtypeStruct(parts[0].shape, jnp.bfloat16),
        in_specs=[VMEM] * (1 + len(parts)),
        out_specs=VMEM,
        compiler_params=pltpu.CompilerParams(vmem_limit_bytes=LIMIT),
        name="add_zones",
    )(taps, *parts)


def filter_kernel(near, taps_ref, *refs):
    values, outs = refs[:near], refs[near:]
    rows = values[0].shape[0]
    together = jnp.concatenate([r[...] for r in values[::-1]], axis=0)
    high = taps_ref[...].astype(jnp.bfloat16)
    low = (taps_ref[...] - high.astype(jnp.float32)).astype(jnp.bfloat16)
    result = jnp.dot(
        jnp.concatenate([high, low], axis=0), together, preferred_element_type=jnp.float32
    )
    result = result[: high.shape[0]] + result[high.shape[0] :]
    if len(outs) == 1:
        outs[0][...] = result.astype(outs[0].dtype)
        return
    for step, out in enumerate(outs):
        out[...] = result[step * rows : (step + 1) * rows].astype(out.dtype)


def time_filter(taps, values):
    rows, cells = values[-1].shape
    steps = taps.shape[0] // rows
    if steps <= DIRECT:
        outs = [
            jax.ShapeDtypeStruct((rows, cells), jnp.bfloat16 if step else jnp.float32)
            for step in range(steps)
        ]
    else:
        outs = [jax.ShapeDtypeStruct((steps * rows, cells), jnp.bfloat16)]
    return pl.pallas_call(
        functools.partial(filter_kernel, len(values)),
        out_shape=outs,
        in_specs=[VMEM] * (1 + len(values)),
        out_specs=[VMEM] * len(outs),
        compiler_params=pltpu.CompilerParams(vmem_limit_bytes=LIMIT),
        name="time_filter",
    )(taps, *values)


def sum_kernel(*refs):
    refs[-1][...] = sum(r[...].astype(jnp.float32) for r in refs[:-1])


def add_up(parts):
    return pl.pallas_call(
        sum_kernel,
        out_shape=jax.ShapeDtypeStruct(parts[0].shape, jnp.float32),
        in_specs=[VMEM] * len(parts),
        out_specs=VMEM,
        compiler_params=pltpu.CompilerParams(vmem_limit_bytes=LIMIT),
        name="add_up",
    )(*parts)


def swap(value, axis, by):
    return lax.ppermute(value, axis, [(i, i ^ by) for i in range(lax.axis_size(axis))])


def swap_both(value, tm_by, zone_by):
    owners, zones = lax.axis_size("tm"), lax.axis_size("zone")
    pairs = [
        (t * zones + z, (t ^ tm_by) * zones + (z ^ zone_by))
        for t in range(owners)
        for z in range(zones)
    ]
    return lax.ppermute(value, ("tm", "zone"), pairs)


def shards(source_field, remap_weights, block_columns, piece_sizes, filter_taps):
    rows, cells = source_field.shape
    zones, owners = lax.axis_size("zone"), lax.axis_size("tm")
    near = min(NEAR, owners)
    steps = owners // near
    where = jnp.stack([lax.axis_index("zone"), lax.axis_index("tm")]).reshape(1, 2)
    xlow = source_field.astype(jnp.bfloat16)
    xs = [xlow] + [swap(xlow, "zone", step) for step in range(zones - 1, 0, -1)]
    held, turned = hold(remap_weights)
    sent = remap(where, block_columns.T, piece_sizes, xs, held, turned)
    taps = prepare(where, filter_taps, steps, near, rows)
    low = add_zones(
        taps, [sent[0]] + [swap(sent[step], "zone", step) for step in range(1, zones)]
    )
    flip = 1 if steps <= DIRECT else 0
    others = [swap_both(low, n, flip) for n in range(near - 1, 0, -1)]
    parts = time_filter(taps, others + [swap(low, "zone", flip) if flip else low])
    if steps <= DIRECT:
        last = [swap_both(parts[step], near * step, flip) for step in range(steps - 1, 0, -1)]
        return add_up(last + [swap(parts[0], "zone", flip)])
    groups = [list(range(side, owners, near)) for side in range(near)]
    parts = lax.all_to_all(
        parts[0].reshape(steps, rows, cells), "tm", 0, 0, axis_index_groups=groups
    )
    return parts.astype(jnp.float32).sum(axis=0)


def solution(mesh):
    return jax.shard_map(
        shards,
        mesh=mesh,
        in_specs=(
            P("tm", "zone"),
            P("zone", None, None, None),
            P("zone", None),
            P("zone", None),
            P(),
        ),
        out_specs=P("tm", "zone"),
        check_vma=False,
    )
```

```python
import functools
import jax
import jax.numpy as jnp
from jax import lax
from jax.experimental import pallas as pl
from jax.experimental.pallas import tpu as pltpu
from jax.sharding import PartitionSpec as P

VMEM = pl.BlockSpec(memory_space=pltpu.VMEM)
HBM = pl.BlockSpec(memory_space=pltpu.HBM)
NT = (((1,), (1,)), ((), ()))
LIMIT = 16 * 2**20
DIRECT = 8
NEAR = 4


def ahead(snapshots, half_width, width):
    return -(-max(0, snapshots + width - half_width) // 128) * 128


def hold_kernel(weights_ref, held_ref, turned_ref, sems):
    zone_blocks, slots, _, _ = weights_ref.shape
    parts = sems.shape[0]
    each = zone_blocks // parts
    copies = [
        pltpu.make_async_copy(
            weights_ref.at[pl.ds(n * each, each)], held_ref.at[pl.ds(n * each, each)], sems.at[n]
        )
        for n in range(parts)
    ]
    for copy in copies:
        copy.start()
    for n, copy in enumerate(copies):
        copy.wait()
        for i in range(n * each, min((n + 1) * each, turned_ref.shape[0])):
            for k in range(slots):
                turned_ref[i, k] = held_ref[i, k].T


def hold(weights):
    zone_blocks = weights.shape[0]
    turned = zone_blocks - zone_blocks // 4
    return pl.pallas_call(
        hold_kernel,
        out_shape=[
            jax.ShapeDtypeStruct((count, *weights.shape[1:]), weights.dtype)
            for count in (zone_blocks, turned)
        ],
        in_specs=[HBM],
        out_specs=[VMEM] * 2,
        scratch_shapes=[pltpu.SemaphoreType.DMA((min(4, weights.shape[0]),))],
        compiler_params=pltpu.CompilerParams(vmem_limit_bytes=43 * 2**20),
        cost_estimate=pl.CostEstimate(flops=0, bytes_accessed=8 * 2**20, transcendentals=0),
        name="hold",
    )(weights)


def prepare_kernel(where_ref, taps_ref, rows_ref, line_ref):
    taps_total = taps_ref.shape[1]
    rows, width = line_ref.shape
    half_width = (taps_total - 1) // 2
    steps = rows_ref.shape[0] // rows
    before = ahead(steps * rows_ref.shape[1], half_width, rows_ref.shape[1])
    line_ref[...] = jnp.zeros_like(line_ref)
    line_ref[:, before : before + taps_total] = jnp.broadcast_to(
        taps_ref[...], (rows, taps_total)
    )
    line = line_ref[...]
    row_ids = lax.broadcasted_iota(jnp.int32, (rows, 1), 0)
    slanted = line
    for r in range(1, rows):
        slanted = jnp.where(row_ids == r, pltpu.roll(line, r, 1), slanted)
    line_ref[...] = slanted
    near = rows_ref.shape[1] // rows
    lanes = lax.broadcasted_iota(jnp.int32, (rows, near * rows), 1)
    at = where_ref[0, 1]
    for step in range(steps):
        target = at ^ (near * step) if steps <= DIRECT else near * step + (at & (near - 1))
        found = jnp.zeros((rows, near * rows), jnp.float32)
        for n in range(near):
            base = ((at ^ n) - target) * rows + half_width - n * rows + before
            first = pl.multiple_of((base >> 7) << 7, 128)
            window = line_ref[:, pl.ds(first, 256)]
            turned = pltpu.roll(window, (256 - (base & 127)) & 255, 1)
            found = jnp.where(lanes >= n * rows, turned[:, : near * rows], found)
        rows_ref[step * rows : (step + 1) * rows, :] = found


def prepare(where, filter_taps, steps, near, rows):
    taps_total = filter_taps.shape[0]
    half_width = (taps_total - 1) // 2
    snapshots = near * steps * rows
    width = ahead(snapshots, half_width, near * rows) + max(taps_total + rows, half_width + snapshots) + 256
    width = -(-width // 128) * 128
    return pl.pallas_call(
        prepare_kernel,
        out_shape=jax.ShapeDtypeStruct((steps * rows, near * rows), jnp.float32),
        in_specs=[VMEM] * 2,
        out_specs=VMEM,
        scratch_shapes=[pltpu.VMEM((rows, width), jnp.float32)],
        compiler_params=pltpu.CompilerParams(vmem_limit_bytes=LIMIT),
        cost_estimate=pl.CostEstimate(flops=0, bytes_accessed=4 * 2**20, transcendentals=0),
        name="prepare",
    )(where, filter_taps.reshape(1, -1))


def remap_kernel(zones, where_ref, columns_ref, sizes_ref, *refs):
    x_refs, (weights_ref, turned_ref, *refs) = refs[:zones], refs[zones:]
    c_refs, (blocks_ref, total_ref) = refs[:zones], refs[zones:]
    zone_blocks, slots, size, _ = weights_ref.shape
    rows = x_refs[0].shape[0]
    me = where_ref[0, 0]
    for step in range(zones):
        first = (me ^ (zones - step if step else 0)) * zone_blocks
        for b in range(zone_blocks):
            blocks_ref[first + b] = x_refs[step][:, b * size : (b + 1) * size].astype(jnp.float32)
    total_ref[...] = jnp.zeros_like(total_ref)

    pieces = []
    for i in range(zone_blocks):
        picked = jnp.concatenate([blocks_ref[columns_ref[k, i]] for k in range(slots)], axis=1)
        picked = picked.astype(jnp.bfloat16)
        if i < turned_ref.shape[0]:
            block = turned_ref[i].reshape(slots * size, size)
            wind = jnp.dot(picked, block, preferred_element_type=jnp.float32)
        else:
            wide = jnp.concatenate([weights_ref[i, k] for k in range(slots)], axis=1)
            wind = lax.dot_general(picked, wide, NT, preferred_element_type=jnp.float32)
        pieces.append(wind * jnp.abs(wind))
    cell_ids = lax.broadcasted_iota(jnp.int32, (rows, size), 1)
    ends = [0]
    for g in range(sizes_ref.shape[1]):
        ends.append(ends[-1] + sizes_ref[0, g])
    totals = [jnp.zeros((rows, size), jnp.float32)] * sizes_ref.shape[1]
    for i, stress in enumerate(pieces):
        ids = cell_ids + i * size
        for g, total in enumerate(totals):
            inside = (ids >= ends[g]) & (ids < ends[g + 1])
            totals[g] = total + jnp.where(inside, stress, 0.0)
    means = [
        jnp.broadcast_to(
            jnp.sum(total, axis=1, keepdims=True) / sizes_ref[0, g].astype(jnp.float32),
            (rows, size),
        )
        for g, total in enumerate(totals)
    ]
    anomalies = []
    for i, stress in enumerate(pieces):
        ids = cell_ids + i * size
        spread = means[0]
        for g in range(1, len(means)):
            spread = jnp.where(ids >= ends[g], means[g], spread)
        anomalies.append(stress - spread)
    anomaly = jnp.concatenate(anomalies, axis=1)

    high = anomaly.astype(jnp.bfloat16)
    low = (anomaly - high.astype(jnp.float32)).astype(jnp.bfloat16)
    both = jnp.concatenate([high, low], axis=0)
    for i in range(zone_blocks):
        wide = jnp.concatenate([weights_ref[i, k] for k in range(slots)], axis=1)
        back = jnp.dot(
            both[:, i * size : (i + 1) * size], wide, preferred_element_type=jnp.float32
        )
        back = back[:rows] + back[rows:]
        targets = [columns_ref[k, i] for k in range(slots)]
        before = [total_ref[column] for column in targets]
        for k in range(slots):
            total_ref[targets[k]] = before[k] + back[:, k * size : (k + 1) * size]
    for step in range(zones):
        first = (me ^ step) * zone_blocks
        for b in range(zone_blocks):
            c_refs[step][:, b * size : (b + 1) * size] = total_ref[first + b].astype(
                c_refs[step].dtype
            )


def remap(where, columns, sizes, xs, weights, turned):
    zones = len(xs)
    rows, cells = xs[0].shape
    all_blocks = zones * weights.shape[0]
    size = weights.shape[2]
    outs = [
        jax.ShapeDtypeStruct((rows, cells), jnp.bfloat16 if step else jnp.float32)
        for step in range(zones)
    ]
    return pl.pallas_call(
        functools.partial(remap_kernel, zones),
        out_shape=outs,
        in_specs=[VMEM] * (5 + zones),
        out_specs=[VMEM] * zones,
        scratch_shapes=[
            pltpu.VMEM((all_blocks, rows, size), jnp.float32),
            pltpu.VMEM((all_blocks, rows, size), jnp.float32),
        ],
        compiler_params=pltpu.CompilerParams(vmem_limit_bytes=LIMIT),
        cost_estimate=pl.CostEstimate(flops=10**8, bytes_accessed=8 * 2**20, transcendentals=0),
        name="remap",
    )(where, columns, sizes, *xs, weights, turned)


def gather_kernel(taps_ref, *refs):
    *parts, low_ref = refs
    del taps_ref
    low_ref[...] = sum(r[...].astype(jnp.float32) for r in parts).astype(low_ref.dtype)


def add_zones(taps, parts):
    return pl.pallas_call(
        gather_kernel,
        out_shape=jax.ShapeDtypeStruct(parts[0].shape, jnp.bfloat16),
        in_specs=[VMEM] * (1 + len(parts)),
        out_specs=VMEM,
        compiler_params=pltpu.CompilerParams(vmem_limit_bytes=LIMIT),
        name="add_zones",
    )(taps, *parts)


def filter_kernel(near, taps_ref, *refs):
    values, outs = refs[:near], refs[near:]
    rows = values[0].shape[0]
    together = jnp.concatenate([r[...] for r in values[::-1]], axis=0)
    high = taps_ref[...].astype(jnp.bfloat16)
    low = (taps_ref[...] - high.astype(jnp.float32)).astype(jnp.bfloat16)
    result = jnp.dot(
        jnp.concatenate([high, low], axis=0), together, preferred_element_type=jnp.float32
    )
    result = result[: high.shape[0]] + result[high.shape[0] :]
    if len(outs) == 1:
        outs[0][...] = result.astype(outs[0].dtype)
        return
    for step, out in enumerate(outs):
        out[...] = result[step * rows : (step + 1) * rows].astype(out.dtype)


def time_filter(taps, values):
    rows, cells = values[-1].shape
    steps = taps.shape[0] // rows
    if steps <= DIRECT:
        outs = [
            jax.ShapeDtypeStruct((rows, cells), jnp.bfloat16 if step else jnp.float32)
            for step in range(steps)
        ]
    else:
        outs = [jax.ShapeDtypeStruct((steps * rows, cells), jnp.bfloat16)]
    return pl.pallas_call(
        functools.partial(filter_kernel, len(values)),
        out_shape=outs,
        in_specs=[VMEM] * (1 + len(values)),
        out_specs=[VMEM] * len(outs),
        compiler_params=pltpu.CompilerParams(vmem_limit_bytes=LIMIT),
        name="time_filter",
    )(taps, *values)


def sum_kernel(*refs):
    refs[-1][...] = sum(r[...].astype(jnp.float32) for r in refs[:-1])


def add_up(parts):
    return pl.pallas_call(
        sum_kernel,
        out_shape=jax.ShapeDtypeStruct(parts[0].shape, jnp.float32),
        in_specs=[VMEM] * len(parts),
        out_specs=VMEM,
        compiler_params=pltpu.CompilerParams(vmem_limit_bytes=LIMIT),
        name="add_up",
    )(*parts)


def swap(value, axis, by):
    return lax.ppermute(value, axis, [(i, i ^ by) for i in range(lax.axis_size(axis))])


def swap_both(value, tm_by, zone_by):
    owners, zones = lax.axis_size("tm"), lax.axis_size("zone")
    pairs = [
        (t * zones + z, (t ^ tm_by) * zones + (z ^ zone_by))
        for t in range(owners)
        for z in range(zones)
    ]
    return lax.ppermute(value, ("tm", "zone"), pairs)


def shards(source_field, remap_weights, block_columns, piece_sizes, filter_taps):
    rows, cells = source_field.shape
    zones, owners = lax.axis_size("zone"), lax.axis_size("tm")
    near = min(NEAR, owners)
    steps = owners // near
    where = jnp.stack([lax.axis_index("zone"), lax.axis_index("tm")]).reshape(1, 2)
    xlow = source_field.astype(jnp.bfloat16)
    xs = [xlow] + [swap(xlow, "zone", step) for step in range(zones - 1, 0, -1)]
    held, turned = hold(remap_weights)
    sent = remap(where, block_columns.T, piece_sizes, xs, held, turned)
    taps = prepare(where, filter_taps, steps, near, rows)
    low = add_zones(
        taps, [sent[0]] + [swap(sent[step], "zone", step) for step in range(1, zones)]
    )
    flip = 1 if steps <= DIRECT else 0
    others = [swap_both(low, n, flip) for n in range(near - 1, 0, -1)]
    parts = time_filter(taps, others + [swap(low, "zone", flip) if flip else low])
    if steps <= DIRECT:
        last = [swap_both(parts[step], near * step, flip) for step in range(steps - 1, 0, -1)]
        return add_up(last + [swap(parts[0], "zone", flip)])
    groups = [list(range(side, owners, near)) for side in range(near)]
    parts = lax.all_to_all(
        parts[0].reshape(steps, rows, cells), "tm", 0, 0, axis_index_groups=groups
    )
    return parts.astype(jnp.float32).sum(axis=0)


def solution(mesh):
    return jax.shard_map(
        shards,
        mesh=mesh,
        in_specs=(
            P("tm", "zone"),
            P("zone", None, None, None),
            P("zone", None),
            P("zone", None),
            P(),
        ),
        out_specs=P("tm", "zone"),
        check_vma=False,
    )
```

```python
import functools
import jax
import jax.numpy as jnp
from jax import lax
from jax.experimental import pallas as pl
from jax.experimental.pallas import tpu as pltpu
from jax.sharding import PartitionSpec as P

VMEM = pl.BlockSpec(memory_space=pltpu.VMEM)
HBM = pl.BlockSpec(memory_space=pltpu.HBM)
NT = (((1,), (1,)), ((), ()))
LIMIT = 16 * 2**20
DIRECT = 8
NEAR = 4


def ahead(snapshots, half_width, width):
    return -(-max(0, snapshots + width - half_width) // 128) * 128


def hold_kernel(weights_ref, held_ref, turned_ref, sems):
    zone_blocks, slots, _, _ = weights_ref.shape
    parts = sems.shape[0]
    each = zone_blocks // parts
    copies = [
        pltpu.make_async_copy(
            weights_ref.at[pl.ds(n * each, each)], held_ref.at[pl.ds(n * each, each)], sems.at[n]
        )
        for n in range(parts)
    ]
    for copy in copies:
        copy.start()
    for n, copy in enumerate(copies):
        copy.wait()
        for i in range(n * each, min((n + 1) * each, turned_ref.shape[0])):
            for k in range(slots):
                turned_ref[i, k] = held_ref[i, k].T


def hold(weights):
    zone_blocks = weights.shape[0]
    turned = zone_blocks - zone_blocks // 4
    return pl.pallas_call(
        hold_kernel,
        out_shape=[
            jax.ShapeDtypeStruct((count, *weights.shape[1:]), weights.dtype)
            for count in (zone_blocks, turned)
        ],
        in_specs=[HBM],
        out_specs=[VMEM] * 2,
        scratch_shapes=[pltpu.SemaphoreType.DMA((min(4, weights.shape[0]),))],
        compiler_params=pltpu.CompilerParams(vmem_limit_bytes=43 * 2**20),
        cost_estimate=pl.CostEstimate(flops=0, bytes_accessed=8 * 2**20, transcendentals=0),
        name="hold",
    )(weights)


def prepare_kernel(where_ref, taps_ref, rows_ref, line_ref):
    taps_total = taps_ref.shape[1]
    rows, width = line_ref.shape
    half_width = (taps_total - 1) // 2
    steps = rows_ref.shape[0] // rows
    before = ahead(steps * rows_ref.shape[1], half_width, rows_ref.shape[1])
    line_ref[...] = jnp.zeros_like(line_ref)
    line_ref[:, before : before + taps_total] = jnp.broadcast_to(
        taps_ref[...], (rows, taps_total)
    )
    line = line_ref[...]
    row_ids = lax.broadcasted_iota(jnp.int32, (rows, 1), 0)
    slanted = line
    for r in range(1, rows):
        slanted = jnp.where(row_ids == r, pltpu.roll(line, r, 1), slanted)
    line_ref[...] = slanted
    near = rows_ref.shape[1] // rows
    lanes = lax.broadcasted_iota(jnp.int32, (rows, near * rows), 1)
    at = where_ref[0, 1]
    for step in range(steps):
        target = at ^ (near * step) if steps <= DIRECT else near * step + (at & (near - 1))
        found = jnp.zeros((rows, near * rows), jnp.float32)
        for n in range(near):
            base = ((at ^ n) - target) * rows + half_width - n * rows + before
            first = pl.multiple_of((base >> 7) << 7, 128)
            window = line_ref[:, pl.ds(first, 256)]
            turned = pltpu.roll(window, (256 - (base & 127)) & 255, 1)
            found = jnp.where(lanes >= n * rows, turned[:, : near * rows], found)
        rows_ref[step * rows : (step + 1) * rows, :] = found


def prepare(where, filter_taps, steps, near, rows):
    taps_total = filter_taps.shape[0]
    half_width = (taps_total - 1) // 2
    snapshots = near * steps * rows
    width = ahead(snapshots, half_width, near * rows) + max(taps_total + rows, half_width + snapshots) + 256
    width = -(-width // 128) * 128
    return pl.pallas_call(
        prepare_kernel,
        out_shape=jax.ShapeDtypeStruct((steps * rows, near * rows), jnp.float32),
        in_specs=[VMEM] * 2,
        out_specs=VMEM,
        scratch_shapes=[pltpu.VMEM((rows, width), jnp.float32)],
        compiler_params=pltpu.CompilerParams(vmem_limit_bytes=LIMIT),
        cost_estimate=pl.CostEstimate(flops=0, bytes_accessed=4 * 2**20, transcendentals=0),
        name="prepare",
    )(where, filter_taps.reshape(1, -1))


def remap_kernel(zones, where_ref, columns_ref, sizes_ref, *refs):
    x_refs, (weights_ref, turned_ref, *refs) = refs[:zones], refs[zones:]
    c_refs, (blocks_ref, total_ref) = refs[:zones], refs[zones:]
    zone_blocks, slots, size, _ = weights_ref.shape
    rows = x_refs[0].shape[0]
    me = where_ref[0, 0]
    for step in range(zones):
        first = (me ^ (zones - step if step else 0)) * zone_blocks
        for b in range(zone_blocks):
            blocks_ref[first + b] = x_refs[step][:, b * size : (b + 1) * size].astype(jnp.float32)
    total_ref[...] = jnp.zeros_like(total_ref)

    pieces = []
    for i in range(zone_blocks):
        picked = jnp.concatenate([blocks_ref[columns_ref[k, i]] for k in range(slots)], axis=1)
        picked = picked.astype(jnp.bfloat16)
        if i < turned_ref.shape[0]:
            block = turned_ref[i].reshape(slots * size, size)
            wind = jnp.dot(picked, block, preferred_element_type=jnp.float32)
        else:
            wide = jnp.concatenate([weights_ref[i, k] for k in range(slots)], axis=1)
            wind = lax.dot_general(picked, wide, NT, preferred_element_type=jnp.float32)
        pieces.append(wind * jnp.abs(wind))
    cell_ids = lax.broadcasted_iota(jnp.int32, (rows, size), 1)
    ends = [0]
    for g in range(sizes_ref.shape[1]):
        ends.append(ends[-1] + sizes_ref[0, g])
    totals = [jnp.zeros((rows, size), jnp.float32)] * sizes_ref.shape[1]
    for i, stress in enumerate(pieces):
        ids = cell_ids + i * size
        for g, total in enumerate(totals):
            inside = (ids >= ends[g]) & (ids < ends[g + 1])
            totals[g] = total + jnp.where(inside, stress, 0.0)
    means = [
        jnp.broadcast_to(
            jnp.sum(total, axis=1, keepdims=True) / sizes_ref[0, g].astype(jnp.float32),
            (rows, size),
        )
        for g, total in enumerate(totals)
    ]
    anomalies = []
    for i, stress in enumerate(pieces):
        ids = cell_ids + i * size
        spread = means[0]
        for g in range(1, len(means)):
            spread = jnp.where(ids >= ends[g], means[g], spread)
        anomalies.append(stress - spread)
    anomaly = jnp.concatenate(anomalies, axis=1)

    high = anomaly.astype(jnp.bfloat16)
    low = (anomaly - high.astype(jnp.float32)).astype(jnp.bfloat16)
    both = jnp.concatenate([high, low], axis=0)
    for i in range(zone_blocks):
        wide = jnp.concatenate([weights_ref[i, k] for k in range(slots)], axis=1)
        back = jnp.dot(
            both[:, i * size : (i + 1) * size], wide, preferred_element_type=jnp.float32
        )
        back = back[:rows] + back[rows:]
        targets = [columns_ref[k, i] for k in range(slots)]
        before = [total_ref[column] for column in targets]
        for k in range(slots):
            total_ref[targets[k]] = before[k] + back[:, k * size : (k + 1) * size]
    for step in range(zones):
        first = (me ^ step) * zone_blocks
        for b in range(zone_blocks):
            c_refs[step][:, b * size : (b + 1) * size] = total_ref[first + b].astype(
                c_refs[step].dtype
            )


def remap(where, columns, sizes, xs, weights, turned):
    zones = len(xs)
    rows, cells = xs[0].shape
    all_blocks = zones * weights.shape[0]
    size = weights.shape[2]
    outs = [
        jax.ShapeDtypeStruct((rows, cells), jnp.bfloat16 if step else jnp.float32)
        for step in range(zones)
    ]
    return pl.pallas_call(
        functools.partial(remap_kernel, zones),
        out_shape=outs,
        in_specs=[VMEM] * (5 + zones),
        out_specs=[VMEM] * zones,
        scratch_shapes=[
            pltpu.VMEM((all_blocks, rows, size), jnp.float32),
            pltpu.VMEM((all_blocks, rows, size), jnp.float32),
        ],
        compiler_params=pltpu.CompilerParams(vmem_limit_bytes=LIMIT),
        cost_estimate=pl.CostEstimate(flops=10**8, bytes_accessed=8 * 2**20, transcendentals=0),
        name="remap",
    )(where, columns, sizes, *xs, weights, turned)


def gather_kernel(taps_ref, *refs):
    *parts, low_ref = refs
    del taps_ref
    low_ref[...] = sum(r[...].astype(jnp.float32) for r in parts).astype(low_ref.dtype)


def add_zones(taps, parts):
    return pl.pallas_call(
        gather_kernel,
        out_shape=jax.ShapeDtypeStruct(parts[0].shape, jnp.bfloat16),
        in_specs=[VMEM] * (1 + len(parts)),
        out_specs=VMEM,
        compiler_params=pltpu.CompilerParams(vmem_limit_bytes=LIMIT),
        name="add_zones",
    )(taps, *parts)


def filter_kernel(near, taps_ref, *refs):
    values, outs = refs[:near], refs[near:]
    rows = values[0].shape[0]
    together = jnp.concatenate([r[...] for r in values[::-1]], axis=0)
    high = taps_ref[...].astype(jnp.bfloat16)
    low = (taps_ref[...] - high.astype(jnp.float32)).astype(jnp.bfloat16)
    result = jnp.dot(
        jnp.concatenate([high, low], axis=0), together, preferred_element_type=jnp.float32
    )
    result = result[: high.shape[0]] + result[high.shape[0] :]
    if len(outs) == 1:
        outs[0][...] = result.astype(outs[0].dtype)
        return
    for step, out in enumerate(outs):
        out[...] = result[step * rows : (step + 1) * rows].astype(out.dtype)


def time_filter(taps, values):
    rows, cells = values[-1].shape
    steps = taps.shape[0] // rows
    if steps <= DIRECT:
        outs = [
            jax.ShapeDtypeStruct((rows, cells), jnp.bfloat16)
            for step in range(steps)
        ]
    else:
        outs = [jax.ShapeDtypeStruct((steps * rows, cells), jnp.bfloat16)]
    return pl.pallas_call(
        functools.partial(filter_kernel, len(values)),
        out_shape=outs,
        in_specs=[VMEM] * (1 + len(values)),
        out_specs=[VMEM] * len(outs),
        compiler_params=pltpu.CompilerParams(vmem_limit_bytes=LIMIT),
        name="time_filter",
    )(taps, *values)


def sum_kernel(*refs):
    refs[-1][...] = sum(r[...].astype(jnp.float32) for r in refs[:-1])


def add_up(parts):
    return pl.pallas_call(
        sum_kernel,
        out_shape=jax.ShapeDtypeStruct(parts[0].shape, jnp.float32),
        in_specs=[VMEM] * len(parts),
        out_specs=VMEM,
        compiler_params=pltpu.CompilerParams(vmem_limit_bytes=LIMIT),
        name="add_up",
    )(*parts)


def swap(value, axis, by):
    return lax.ppermute(value, axis, [(i, i ^ by) for i in range(lax.axis_size(axis))])


def swap_both(value, tm_by, zone_by):
    owners, zones = lax.axis_size("tm"), lax.axis_size("zone")
    pairs = [
        (t * zones + z, (t ^ tm_by) * zones + (z ^ zone_by))
        for t in range(owners)
        for z in range(zones)
    ]
    return lax.ppermute(value, ("tm", "zone"), pairs)


def shards(source_field, remap_weights, block_columns, piece_sizes, filter_taps):
    rows, cells = source_field.shape
    zones, owners = lax.axis_size("zone"), lax.axis_size("tm")
    near = min(NEAR, owners)
    steps = owners // near
    where = jnp.stack([lax.axis_index("zone"), lax.axis_index("tm")]).reshape(1, 2)
    xlow = source_field.astype(jnp.bfloat16)
    xs = [xlow] + [swap(xlow, "zone", step) for step in range(zones - 1, 0, -1)]
    held, turned = hold(remap_weights)
    sent = remap(where, block_columns.T, piece_sizes, xs, held, turned)
    taps = prepare(where, filter_taps, steps, near, rows)
    low = add_zones(
        taps, [sent[0]] + [swap(sent[step], "zone", step) for step in range(1, zones)]
    )
    flip = 1 if steps <= DIRECT else 0
    others = [swap_both(low, n, flip) for n in range(near - 1, 0, -1)]
    parts = time_filter(taps, others + [swap(low, "zone", flip) if flip else low])
    if steps <= DIRECT:
        last = [swap_both(parts[step], near * step, flip) for step in range(steps - 1, 0, -1)]
        return add_up(last + [swap(parts[0], "zone", flip)])
    groups = [list(range(side, owners, near)) for side in range(near)]
    parts = lax.all_to_all(
        parts[0].reshape(steps, rows, cells), "tm", 0, 0, axis_index_groups=groups
    )
    return parts.astype(jnp.float32).sum(axis=0)


def solution(mesh):
    return jax.shard_map(
        shards,
        mesh=mesh,
        in_specs=(
            P("tm", "zone"),
            P("zone", None, None, None),
            P("zone", None),
            P("zone", None),
            P(),
        ),
        out_specs=P("tm", "zone"),
        check_vma=False,
    )
```
